256 devices in a mesh: prow: 16 (over y, x), pcol: 16 (over z, core).
Axes of the slice: x: 4, y: 4, z: 8, core: 2. Of those that a mesh axis runs over, the one named last changes fastest.
Arguments:
- inverse_region: bfloat16 [8, 4096, 8, 4096], P(None, 'prow', None, 'pcol'), may hold values from -5 to 5
- panel_one: bfloat16 [16384, 256], P('pcol'), may hold values from -0.046875 to 0.046875
- panel_two: bfloat16 [8192, 256], P('pcol'), may hold values from -0.0625 to 0.0625
- link_block: bfloat16 [256, 256], replicated, may hold values from -0.375 to 0.375
- inv_diag_one: float32 [256, 256], replicated, may hold values from -5 to 5
- inv_diag_two: float32 [256, 256], replicated, may hold values from -5 to 5
- pattern_one: int32 [64], replicated, may hold values from 0 to 127, as said below
- pattern_two: int32 [32], replicated, may hold values from 0 to 127, as said below
Outputs:
- column_one: bfloat16 [8, 4096, 256], P(None, ('prow', 'pcol'))
- diagonal_one: float32 [256, 256], replicated
- column_two: bfloat16 [8, 4096, 256], P(None, ('prow', 'pcol'))
- cross_two: float32 [256, 256], replicated
- diagonal_two: float32 [256, 256], replicated
The draws below stay inside these ranges and needn't reach their ends.
Inputs may be any that keep to these rules, and one draw needn't show every extreme that they name: `pattern_one`: 64 distinct indices in increasing order; the first block 0 and the top block 127 are always among them. `pattern_two`: 32 distinct entries of pattern_one in increasing order; the first and the last entry of pattern_one are always among them.
All inputs are finite; a program needn't handle non-finite values.
Results may differ from the reference program's by a relative error of at most 0.004.
Values may be sent and summed in bfloat16 or wider, within the bound.
No kernel may reach another device: no remote copies, remote signals or barrier semaphores. Data moves between devices by JAX's collectives and lax.ppermute only.
A program may use at most 128 MiB of HBM per device.

```python
import jax
import jax.numpy as jnp
from jax import lax

B = 256
ROWB = 8
NB = 128
COLB = 8
S1 = 64
S2 = 32
N_PROW = 16
N_PCOL = 16


def choose_blocks(key):
    places = jnp.arange(NB, dtype=jnp.int32)
    ranking = jax.random.randint(key, (NB,), 0, 2 * NB, dtype=jnp.int32) + places
    ranking = jnp.where((places == NB - 1) | (places == 0), 8 * NB, ranking)
    scores = ranking * (2 * NB) + places
    chosen = lax.top_k(scores, S1)[1].astype(jnp.int32)
    leading = jnp.sort(chosen)
    middle = jax.random.permutation(jax.random.fold_in(key, 7), S1 - 2)[:S2 - 2].astype(jnp.int32) + 1
    ends_low = jnp.zeros((1,), jnp.int32)
    ends_high = jnp.full((1,), S1 - 1, jnp.int32)
    subset_pos = jnp.concatenate([ends_low, middle, ends_high])
    trailing = jnp.sort(leading[subset_pos])
    return (leading, trailing)


def draw_pattern_one(key, part):
    return choose_blocks(key)[0].astype(jnp.int32)


def draw_pattern_two(key, part):
    return choose_blocks(key)[1].astype(jnp.int32)


def levels(stream_key, shape, pieces, least, high):
    level, own = 1.0, jax.random.fold_in(stream_key, 6)
    for axis_at, shards_of in pieces:
        heights = jnp.exp(jax.random.uniform(jax.random.fold_in(own, axis_at), (shards_of,), jnp.float32, least / len(pieces), high / len(pieces)))
        level = level * jnp.repeat(heights, shape[axis_at] // shards_of).reshape([-1 if axis == axis_at else 1 for axis in range(len(shape))])
    return level


def noise(own_key, shape, width, limit, shards=(), kind=jnp.bfloat16):
    entries = jax.random.normal(own_key, shape, jnp.float32) * width
    if len(shards) > 0:
        entries = levels(own_key, shape, shards, -0.22, 0.18) * entries
    return jnp.clip(entries, min=-limit, max=limit).astype(kind)


def setup_inputs(seed: int = 0) -> dict:
    key_list = jax.random.split(jax.random.key(seed), 9)
    return {
        "inverse_region": noise(key_list[0], (ROWB, N_PROW * B, COLB, N_PCOL * B), 1.0, 5.0, ((1, 16), (3, 16))),
        "panel_one": noise(key_list[1], (S1 * B, B), (S1 * B) ** -0.5, 0.046875, ((0, 16),)),
        "panel_two": noise(key_list[2], (S2 * B, B), (S2 * B) ** -0.5, 0.0625, ((0, 16),)),
        "link_block": noise(key_list[3], (B, B), B ** -0.5, 0.375),
        "inv_diag_one": noise(key_list[4], (B, B), 1.0, 5.0, (), jnp.float32),
        "inv_diag_two": noise(key_list[5], (B, B), 1.0, 5.0, (), jnp.float32),
        "pattern_one": draw_pattern_one(jax.random.fold_in(key_list[8], 71), 0),
        "pattern_two": draw_pattern_two(jax.random.fold_in(key_list[8], 71), 0),
    }


def reference(inverse_region, panel_one, panel_two, link_block, inv_diag_one, inv_diag_two, pattern_one, pattern_two):
    square = inverse_region.reshape(NB, B, NB, B)
    minor_one = square[pattern_one][:, :, pattern_one].reshape(S1 * B, S1 * B)
    product_one = jnp.dot(minor_one, panel_one, preferred_element_type=jnp.float32)
    packed_one = (-product_one).astype(jnp.bfloat16).reshape(S1, B, B)
    blocks_one = panel_one.reshape(S1, B, B).astype(jnp.float32)
    diagonal_one = inv_diag_one - jnp.einsum("sij,sik->jk", blocks_one, packed_one.astype(jnp.float32))
    full_one = jnp.zeros((NB, B, B), jnp.bfloat16).at[pattern_one].set(packed_one)
    column_one = full_one.reshape(ROWB, N_PROW * B, B)
    minor_two = square[pattern_two][:, :, pattern_two].reshape(S2 * B, S2 * B)
    above = full_one[pattern_two]
    product_two = jnp.dot(minor_two, panel_two, preferred_element_type=jnp.float32)
    product_two = product_two + jnp.dot(above.reshape(S2 * B, B), link_block, preferred_element_type=jnp.float32)
    packed_two = (-product_two).astype(jnp.bfloat16).reshape(S2, B, B)
    column_two = jnp.zeros((NB, B, B), jnp.bfloat16).at[pattern_two].set(packed_two).reshape(ROWB, N_PROW * B, B)
    blocks_two = panel_two.reshape(S2, B, B).astype(jnp.float32)
    link_float = link_block.astype(jnp.float32)
    cross_two = -jnp.dot(diagonal_one, link_float, precision=lax.Precision.HIGHEST) - jnp.einsum("sij,sik->jk", above.astype(jnp.float32), blocks_two)
    diagonal_two = inv_diag_two - jnp.einsum("sij,sik->jk", blocks_two, packed_two.astype(jnp.float32))
    diagonal_two = diagonal_two - jnp.dot(link_float.T, cross_two, precision=lax.Precision.HIGHEST)
    return column_one, diagonal_one, column_two, cross_two, diagonal_two
```

```python
import jax
import jax.numpy as jnp
from jax import lax
from jax.experimental import pallas as pl
from jax.experimental.pallas import tpu as pltpu
from jax.sharding import PartitionSpec as P

BF16 = jnp.bfloat16
F32 = jnp.float32
VMEM = pl.BlockSpec(memory_space=pltpu.VMEM)
SMEM = pl.BlockSpec(memory_space=pltpu.SMEM)
ANY = pl.BlockSpec(memory_space=pl.ANY)
CHIPS = 8
CORES = 2
ROWS = 16
LANES = 128


def params():
    return pltpu.CompilerParams(vmem_limit_bytes=48 * 1024 * 1024)


def places(block_ids, pattern):
    hits = block_ids[:, None] == pattern[None, :]
    at = jnp.arange(pattern.shape[0], dtype=jnp.int32)[None, :] + 1
    return jnp.sum(jnp.where(hits, at, 0), axis=1) - 1


def pick_kernel(slot_ref, gathered_ref, send_ref, own_ref):
    slots = own_ref.shape[0]
    for t in range(slots):
        at = slot_ref[t]
        block = gathered_ref[jnp.maximum(at, 0)]
        block = jnp.where(at >= 0, block, jnp.zeros_like(block))
        own_ref[t] = block
        for d in range(send_ref.shape[0]):
            send_ref[d, t] = block


def pick(slot_at, gathered, peers):
    slots = slot_at.shape[0]
    tail = gathered.shape[1:]
    return pl.pallas_call(
        pick_kernel,
        out_shape=(
            jax.ShapeDtypeStruct((peers, slots) + tail, BF16),
            jax.ShapeDtypeStruct((slots,) + tail, BF16),
        ),
        in_specs=[SMEM, VMEM],
        out_specs=(VMEM, VMEM),
        compiler_params=params(),
        name="pick",
    )(slot_at, gathered)


def product_kernel(
    row_ref, core_ref, region_ref, panel_ref, keep_ref, send_ref,
    region, panel, wide, turned, total, region_sem, panel_sem,
):
    blocks = region.shape[0]
    width = region.shape[1]
    peers = panel_ref.shape[0]
    core = core_ref[0]

    def region_copy(a):
        return pltpu.make_async_copy(region_ref.at[a], region.at[a], region_sem.at[a])

    def panel_copy(p):
        return pltpu.make_async_copy(
            panel_ref.at[p], panel.at[:, pl.ds(p * ROWS, ROWS), :], panel_sem.at[p]
        )

    for p in range(peers):
        panel_copy(p).start()
    for a in range(blocks):
        @pl.when(row_ref[a] >= 0)
        def _():
            region_copy(a).start()
    for p in range(peers):
        panel_copy(p).wait()

    def step(a, carry):
        @pl.when(row_ref[a] >= 0)
        def _():
            region_copy(a).wait()
            for h in range(width // LANES):
                lanes = pl.ds(h * LANES, LANES)
                wide[h] = region[a, :, :, lanes].reshape(width * blocks, LANES).astype(F32)
            for c in range(blocks):
                for h in range(width // LANES):
                    turned[:, pl.ds(c * width + h * LANES, LANES)] = wide[
                        h, pl.ds(c, width, stride=blocks), :
                    ].astype(BF16)
            first = panel[:blocks].reshape(blocks * width, width)
            one = jnp.dot(turned[...], first, preferred_element_type=F32)
            total[:, :, :, :width] = one.reshape(CHIPS, CORES, ROWS, width)

            @pl.when(row_ref[blocks + a] >= 0)
            def _():
                second = panel[blocks:].reshape(blocks * width, width)
                two = jnp.dot(turned[...], second, preferred_element_type=F32)
                total[:, :, :, width:] = two.reshape(CHIPS, CORES, ROWS, width)

            @pl.when(row_ref[blocks + a] < 0)
            def _():
                total[:, :, :, width:] = jnp.zeros((CHIPS, CORES, ROWS, width), F32)

            keep_ref[:, a] = total[:, core]
            send_ref[:, a] = total[:, 1 - core].astype(BF16)

        @pl.when(row_ref[a] < 0)
        def _():
            keep_ref[:, a] = jnp.zeros((CHIPS, ROWS, 2 * width), F32)
            send_ref[:, a] = jnp.zeros((CHIPS, ROWS, 2 * width), BF16)

        return carry

    lax.fori_loop(0, blocks, step, 0)


def product(row_at, core, region, panel):
    blocks, width = region.shape[:2]
    peers, slots = panel.shape[:2]
    return pl.pallas_call(
        product_kernel,
        out_shape=(
            jax.ShapeDtypeStruct((CHIPS, blocks, ROWS, 2 * width), F32),
            jax.ShapeDtypeStruct((CHIPS, blocks, ROWS, 2 * width), BF16),
        ),
        in_specs=[SMEM, SMEM, ANY, ANY],
        out_specs=(VMEM, VMEM),
        scratch_shapes=[
            pltpu.VMEM((blocks, width, blocks, width), BF16),
            pltpu.VMEM((slots, width, width), BF16),
            pltpu.VMEM((width // LANES, width * blocks, LANES), F32),
            pltpu.VMEM((width, blocks * width), BF16),
            pltpu.VMEM((CHIPS, CORES, ROWS, 2 * width), F32),
            pltpu.SemaphoreType.DMA((blocks,)),
            pltpu.SemaphoreType.DMA((peers,)),
        ],
        compiler_params=params(),
        name="product",
    )(row_at, core, region, panel)


def across(a, b):
    return lax.dot_general(a, b, (((0,), (0,)), ((), ())), preferred_element_type=F32)


def columns_kernel(row_ref, parts_ref, rows_ref, link_ref, one_ref, two_ref, sums_ref):
    blocks, share, width = one_ref.shape
    link = link_ref[...]
    total = parts_ref[0].astype(F32)
    for z in range(1, parts_ref.shape[0]):
        total = total + parts_ref[z].astype(F32)
    ones, twos = [], []
    for a in range(blocks):
        first = jnp.where(row_ref[a] >= 0, -total[a, :, :width], 0.0).astype(BF16)
        ones.append(first)
        one_ref[a] = first
    one = jnp.concatenate(ones, axis=0)
    linked = jnp.dot(one, link, preferred_element_type=F32).reshape(blocks, share, width)
    for a in range(blocks):
        second = -(total[a, :, width:] + linked[a])
        second = jnp.where(row_ref[blocks + a] >= 0, second, 0.0).astype(BF16)
        twos.append(second)
        two_ref[a] = second
    two = jnp.concatenate(twos, axis=0)
    rows_one = rows_ref[:blocks].reshape(blocks * share, width)
    rows_two = rows_ref[blocks:].reshape(blocks * share, width)
    sums_ref[:width] = across(rows_one, one).astype(sums_ref.dtype)
    sums_ref[width:2 * width] = across(one, rows_two).astype(sums_ref.dtype)
    sums_ref[2 * width:] = across(rows_two, two).astype(sums_ref.dtype)


def columns(row_at, parts, rows, link):
    blocks, share, wide = parts.shape[1:]
    width = wide // 2
    return pl.pallas_call(
        columns_kernel,
        out_shape=(
            jax.ShapeDtypeStruct((blocks, share, width), BF16),
            jax.ShapeDtypeStruct((blocks, share, width), BF16),
            jax.ShapeDtypeStruct((3 * width, width), BF16),
        ),
        in_specs=[SMEM, VMEM, VMEM, VMEM],
        out_specs=(VMEM, VMEM, VMEM),
        compiler_params=params(),
        name="columns",
    )(row_at, parts, rows, link)


def exact(a, b, dims):
    return lax.dot_general(
        a, b, (dims, ((), ())), precision=lax.Precision.HIGHEST, preferred_element_type=F32
    )


def diagonals_kernel(sums_ref, link_ref, inv_one_ref, inv_two_ref, one_ref, cross_ref, two_ref):
    width = link_ref.shape[0]
    link = link_ref[...].astype(F32)
    one = inv_one_ref[...] - sums_ref[:width].astype(F32)
    one_ref[...] = one
    cross = -exact(one, link, ((1,), (0,))) - sums_ref[width:2 * width].astype(F32)
    cross_ref[...] = cross
    two = inv_two_ref[...] - sums_ref[2 * width:].astype(F32)
    two_ref[...] = two - exact(link, cross, ((0,), (0,)))


def diagonals(sums, link, inv_one, inv_two):
    square = jax.ShapeDtypeStruct(inv_one.shape, F32)
    return pl.pallas_call(
        diagonals_kernel,
        out_shape=(square, square, square),
        in_specs=[VMEM] * 4,
        out_specs=(VMEM,) * 3,
        compiler_params=params(),
        name="diagonals",
    )(sums, link, inv_one, inv_two)


def swap_axes(value, axes, groups=None):
    return lax.all_to_all(value, axes, 0, 0, axis_index_groups=groups, tiled=True)


def sum_everywhere(sums, rows_grid, cols_grid):
    both = ("prow", "pcol")
    planes = [
        [p * cols_grid + z * CORES + c for p in range(rows_grid) for c in range(CORES)]
        for z in range(CHIPS)
    ]
    lines = [[z * CORES + c for z in range(CHIPS)] for c in range(CORES)]
    ways = rows_grid * CORES
    height, width = sums.shape
    share = height // ways
    pieces = swap_axes(sums.reshape(ways, share, width), both, planes)
    piece = jnp.sum(pieces.astype(F32), axis=0)
    pieces = swap_axes(jnp.broadcast_to(piece, (CHIPS, share, width)), "pcol", lines)
    piece = jnp.sum(pieces, axis=0).astype(BF16)
    pieces = swap_axes(jnp.broadcast_to(piece, (ways, share, width)), both, planes)
    return pieces.reshape(height, width)


def shards(
    inverse_region, panel_one, panel_two, link_block, inv_diag_one, inv_diag_two,
    pattern_one, pattern_two,
):
    rows_grid = lax.axis_size("prow")
    cols_grid = lax.axis_size("pcol")
    p = lax.axis_index("prow")
    q = lax.axis_index("pcol")
    blocks, width = inverse_region.shape[:2]
    steps = jnp.arange(blocks, dtype=jnp.int32)
    row_ids = steps * rows_grid + p
    col_ids = steps * cols_grid + q
    row_at = jnp.concatenate([places(row_ids, pattern_one), places(row_ids, pattern_two)])
    held_one = panel_one.shape[0] // width
    held_two = panel_two.shape[0] // width
    held = held_one + held_two
    at_one = places(col_ids, pattern_one)
    at_two = places(col_ids, pattern_two)
    slot_at = jnp.concatenate([
        jnp.where(at_one < 0, -1, (at_one // held_one) * held + at_one % held_one),
        jnp.where(at_two < 0, -1, (at_two // held_two) * held + held_one + at_two % held_two),
    ])

    def own_rows(panel, count):
        return lax.dynamic_slice_in_dim(panel.reshape(count, width, width), p * ROWS, ROWS, 1)

    mine = jnp.concatenate([own_rows(panel_one, held_one), own_rows(panel_two, held_two)], axis=0)
    gathered = lax.all_gather(mine, "pcol", axis=0, tiled=True)
    send, own = pick(slot_at, gathered, rows_grid)
    turn = [(a * cols_grid + b, b * cols_grid + a) for a in range(rows_grid) for b in range(cols_grid)]
    rows = lax.ppermute(own, ("prow", "pcol"), turn)
    panel = swap_axes(send, "prow")
    core = lax.rem(q, CORES).reshape(1)
    keep, give = product(row_at, core, inverse_region, panel)
    got = lax.ppermute(give, "pcol", [(i, i ^ 1) for i in range(cols_grid)])
    paired = (keep + got.astype(F32)).astype(BF16)
    lines = [[z * CORES + c for z in range(CHIPS)] for c in range(CORES)]
    parts = swap_axes(paired, "pcol", lines)
    column_one, column_two, sums = columns(row_at, parts, rows, link_block)
    sums = sum_everywhere(sums, rows_grid, cols_grid)
    diagonal_one, cross_two, diagonal_two = diagonals(sums, link_block, inv_diag_one, inv_diag_two)
    return (column_one, diagonal_one, column_two, cross_two, diagonal_two)


def solution(mesh):
    return jax.shard_map(
        shards,
        mesh=mesh,
        in_specs=(P(None, "prow", None, "pcol"), P("pcol", None), P("pcol", None), P(), P(), P(), P(), P()),
        out_specs=(P(None, ("prow", "pcol"), None), P(), P(None, ("prow", "pcol"), None), P(), P()),
        check_vma=False,
    )
```

```python
import functools

import jax
import jax.numpy as jnp
from jax import lax
from jax.experimental import pallas as pl
from jax.experimental.pallas import tpu as pltpu
from jax.sharding import PartitionSpec as P

BF16 = jnp.bfloat16
F32 = jnp.float32
VMEM = pl.BlockSpec(memory_space=pltpu.VMEM)
SMEM = pl.BlockSpec(memory_space=pltpu.SMEM)
ANY = pl.BlockSpec(memory_space=pl.ANY)
CHIPS = 8
CORES = 2
ROWS = 16
LANES = 128


def params(mebibytes=16):
    return pltpu.CompilerParams(vmem_limit_bytes=mebibytes * 1024 * 1024)


BLOCKS = 8
GROUPS = 4
SECOND_AT = GROUPS * BLOCKS
SPARE = SECOND_AT + BLOCKS
LISTS = SPARE + 1


def pick_kernel(caps, here_ref, one_ref, two_ref, gathered_ref, send_ref, own_ref, lists_ref, found, send_sem):
    grid = send_ref.shape[0]
    held = gathered_ref.shape[0] // grid
    for i in range(LISTS):
        found[i] = -1
        lists_ref[i] = -1
    row, column = here_ref[0], here_ref[1]
    for group, pattern in enumerate((one_ref, two_ref)):
        for s in range(pattern.shape[0]):
            block = pattern[s]
            home, at = lax.rem(block, grid), lax.div(block, grid)
            found[jnp.where(home == column, group * BLOCKS + at, SPARE)] = s
            found[jnp.where(home == row, (2 + group) * BLOCKS + at, SPARE)] = s
    for group in range(GROUPS):
        count = jnp.int32(0)
        for at in range(BLOCKS):
            present = found[group * BLOCKS + at] >= 0
            lists_ref[jnp.where(present, group * BLOCKS + count, SPARE)] = at
            if group == GROUPS - 1:
                lists_ref[SECOND_AT + at] = jnp.where(present, count, -1)
            count = count + present.astype(jnp.int32)
    offset, slot = 0, 0
    for group, pattern in enumerate((one_ref, two_ref)):
        each = pattern.shape[0] // grid
        for t in range(caps[group]):
            at = lists_ref[group * BLOCKS + t]
            s = jnp.where(at >= 0, found[group * BLOCKS + jnp.maximum(at, 0)], 0)
            block = gathered_ref[lax.div(s, each) * held + offset + lax.rem(s, each)]
            own_ref[slot] = jnp.where(at >= 0, block, jnp.zeros_like(block))
            slot += 1
        offset += each
    copies = [pltpu.make_async_copy(own_ref, send_ref.at[d], send_sem.at[d]) for d in range(grid)]
    for copy in copies:
        copy.start()
    for copy in copies:
        copy.wait()


def pick(caps, here, pattern_one, pattern_two, gathered, peers):
    tail = gathered.shape[1:]
    slots = sum(caps)
    return pl.pallas_call(
        functools.partial(pick_kernel, caps),
        out_shape=(
            jax.ShapeDtypeStruct((peers, slots) + tail, BF16),
            jax.ShapeDtypeStruct((slots,) + tail, BF16),
            jax.ShapeDtypeStruct((LISTS,), jnp.int32),
        ),
        in_specs=[SMEM, SMEM, SMEM, VMEM],
        out_specs=(ANY, VMEM, SMEM),
        scratch_shapes=[pltpu.SMEM((LISTS,), jnp.int32), pltpu.SemaphoreType.DMA((peers,))],
        compiler_params=params(),
        name="pick",
    )(here, pattern_one, pattern_two, gathered)


def turn_kernel(caps, lists_ref, region_ref, one_ref, two_ref, region, wide, region_sem):
    width = region.shape[1]
    halves = width // LANES

    def region_copy(u):
        at = lists_ref[2 * BLOCKS + u]
        return pltpu.make_async_copy(region_ref.at[at], region.at[u], region_sem.at[u])

    def each(u, work):
        pl.when(lists_ref[2 * BLOCKS + u] >= 0)(work)

    def place(out_ref, u, group):
        for t in range(caps[group]):
            c = lists_ref[group * BLOCKS + t]
            for h in range(halves):
                lanes = pl.ds(t * width + h * LANES, LANES)

                @pl.when(c >= 0)
                def _():
                    out_ref[u, :, lanes] = wide[h, pl.ds(c, width, stride=BLOCKS), :].astype(BF16)

                @pl.when(c < 0)
                def _():
                    out_ref[u, :, lanes] = jnp.zeros((width, LANES), BF16)

    for u in range(caps[0]):
        each(u, lambda u=u: region_copy(u).start())

    def step(u, carry):
        def work():
            region_copy(u).wait()
            for h in range(halves):
                part = region[u, :, :, pl.ds(h * LANES, LANES)]
                wide[h] = part.reshape(width * BLOCKS, LANES).astype(F32)
            place(one_ref, u, 0)
            second = lists_ref[SECOND_AT + lists_ref[2 * BLOCKS + u]]
            pl.when(second >= 0)(lambda: place(two_ref, second, 1))

        each(u, work)
        return carry

    lax.fori_loop(0, caps[0], step, 0)


def turn(caps, lists, region):
    blocks, width = region.shape[:2]
    return pl.pallas_call(
        functools.partial(turn_kernel, caps),
        out_shape=tuple(jax.ShapeDtypeStruct((k, width, k * width), BF16) for k in caps),
        in_specs=[SMEM, ANY],
        out_specs=(VMEM, VMEM),
        scratch_shapes=[
            pltpu.VMEM((blocks, width, blocks, width), BF16),
            pltpu.VMEM((width // LANES, width * blocks, LANES), F32),
            pltpu.SemaphoreType.DMA((blocks,)),
        ],
        compiler_params=params(20),
        cost_estimate=pl.CostEstimate(flops=2**20, bytes_accessed=2**24, transcendentals=0),
        name="turn",
    )(lists, region)


def product_kernel(
    caps, lists_ref, core_ref, one_ref, two_ref, panel_ref, keep_ref, send_ref, panel, total, panel_sem,
):
    width = one_ref.shape[1]
    peers = panel_ref.shape[0]
    core = core_ref[0]
    copies = [
        pltpu.make_async_copy(panel_ref.at[p], panel.at[:, pl.ds(p * ROWS, ROWS), :], panel_sem.at[p])
        for p in range(peers)
    ]
    for copy in copies:
        copy.start()
    for copy in copies:
        copy.wait()
    first = 0
    for group, turned in enumerate((one_ref, two_ref)):
        cap = caps[group]

        def step(u, carry, group=group, turned=turned, cap=cap, first=first):
            present = lists_ref[(2 + group) * BLOCKS + u] >= 0

            @pl.when(present)
            def _():
                blocks = panel[first:first + cap].reshape(cap * width, width)
                sums = jnp.dot(turned[u], blocks, preferred_element_type=F32)
                total[...] = sums.reshape(total.shape)
                keep_ref[:, first + u] = total[:, core]
                send_ref[:, first + u] = total[:, 1 - core].astype(BF16)

            @pl.when(jnp.logical_not(present))
            def _():
                keep_ref[:, first + u] = jnp.zeros((CHIPS, ROWS, width), F32)
                send_ref[:, first + u] = jnp.zeros((CHIPS, ROWS, width), BF16)

            return carry

        lax.fori_loop(0, cap, step, 0)
        first += cap


def product(caps, lists, core, one, two, panel):
    width = one.shape[1]
    peers, slots = panel.shape[:2]
    shape = (CHIPS, slots, ROWS, width)
    return pl.pallas_call(
        functools.partial(product_kernel, caps),
        out_shape=(jax.ShapeDtypeStruct(shape, F32), jax.ShapeDtypeStruct(shape, BF16)),
        in_specs=[SMEM, SMEM, VMEM, VMEM, ANY],
        out_specs=(VMEM, VMEM),
        scratch_shapes=[
            pltpu.VMEM((slots, width, width), BF16),
            pltpu.VMEM((CHIPS, CORES, ROWS, width), F32),
            pltpu.SemaphoreType.DMA((peers,)),
        ],
        compiler_params=params(),
        name="product",
    )(lists, core, one, two, panel)


def across(a, b):
    return lax.dot_general(a, b, (((0,), (0,)), ((), ())), preferred_element_type=F32)


def columns_kernel(caps, lists_ref, parts_ref, rows_ref, link_ref, one_ref, two_ref, sums_ref, sums, rows):
    blocks, share, width = one_ref.shape
    rows[...] = jnp.zeros(rows.shape, BF16)
    sums[...] = jnp.zeros(sums.shape, F32)
    slot = 0
    for group in range(2):
        for u in range(caps[group]):
            at = lists_ref[(2 + group) * BLOCKS + u]

            @pl.when(at >= 0)
            def _(slot=slot, group=group, at=at):
                total = parts_ref[0, slot].astype(F32)
                for z in range(1, parts_ref.shape[0]):
                    total = total + parts_ref[z, slot].astype(F32)
                place = pl.ds(pl.multiple_of(at * share, share), share)
                sums[group, place] = -total
                rows[group, place] = rows_ref[slot]

            slot += 1
    one = sums[0].astype(BF16)
    one_ref[...] = one.reshape(one_ref.shape)
    linked = jnp.dot(one, link_ref[...], preferred_element_type=F32)
    second = sums[1] - linked
    for at in range(blocks):
        part = slice(at * share, (at + 1) * share)
        kept = jnp.where(lists_ref[SECOND_AT + at] >= 0, second[part], 0.0)
        two_ref[at] = kept.astype(BF16)
    two = two_ref[...].reshape(blocks * share, width)
    kind = sums_ref.dtype
    sums_ref[:width] = across(rows[0], one).astype(kind)
    sums_ref[width:2 * width] = across(one, rows[1]).astype(kind)
    sums_ref[2 * width:] = across(rows[1], two).astype(kind)


def columns(caps, lists, parts, rows, link):
    share, width = parts.shape[2:]
    column = jax.ShapeDtypeStruct((BLOCKS, share, width), BF16)
    return pl.pallas_call(
        functools.partial(columns_kernel, caps),
        out_shape=(column, column, jax.ShapeDtypeStruct((3 * width, width), BF16)),
        in_specs=[SMEM, VMEM, VMEM, VMEM],
        out_specs=(VMEM, VMEM, VMEM),
        scratch_shapes=[
            pltpu.VMEM((2, BLOCKS * share, width), F32),
            pltpu.VMEM((2, BLOCKS * share, width), BF16),
        ],
        compiler_params=params(),
        name="columns",
    )(lists, parts, rows, link)


def exact(a, b, dims):
    return lax.dot_general(
        a, b, (dims, ((), ())), precision=lax.Precision.HIGHEST, preferred_element_type=F32
    )


def diagonals_kernel(sums_ref, link_ref, inv_one_ref, inv_two_ref, one_ref, cross_ref, two_ref):
    width = link_ref.shape[0]
    link = link_ref[...].astype(F32)
    one = inv_one_ref[...] - sums_ref[:width].astype(F32)
    one_ref[...] = one
    cross = -exact(one, link, ((1,), (0,))) - sums_ref[width:2 * width].astype(F32)
    cross_ref[...] = cross
    two = inv_two_ref[...] - sums_ref[2 * width:].astype(F32)
    two_ref[...] = two - exact(link, cross, ((0,), (0,)))


def diagonals(sums, link, inv_one, inv_two):
    square = jax.ShapeDtypeStruct(inv_one.shape, F32)
    return pl.pallas_call(
        diagonals_kernel,
        out_shape=(square, square, square),
        in_specs=[VMEM] * 4,
        out_specs=(VMEM,) * 3,
        compiler_params=params(),
        name="diagonals",
    )(sums, link, inv_one, inv_two)


def swap_axes(value, axes, groups=None):
    return lax.all_to_all(value, axes, 0, 0, axis_index_groups=groups, tiled=True)


def sum_everywhere(sums, rows_grid, cols_grid):
    both = ("prow", "pcol")
    planes = [
        [p * cols_grid + z * CORES + c for p in range(rows_grid) for c in range(CORES)]
        for z in range(CHIPS)
    ]
    lines = [[z * CORES + c for z in range(CHIPS)] for c in range(CORES)]
    ways = rows_grid * CORES
    height, width = sums.shape
    share = height // ways
    pieces = swap_axes(sums.reshape(ways, share, width), both, planes)
    piece = jnp.sum(pieces.astype(F32), axis=0)
    pieces = swap_axes(jnp.broadcast_to(piece, (CHIPS, share, width)), "pcol", lines)
    piece = jnp.sum(pieces, axis=0).astype(BF16)
    pieces = swap_axes(jnp.broadcast_to(piece, (ways, share, width)), both, planes)
    return pieces.reshape(height, width)


def shards(
    inverse_region, panel_one, panel_two, link_block, inv_diag_one, inv_diag_two,
    pattern_one, pattern_two,
):
    rows_grid = lax.axis_size("prow")
    cols_grid = lax.axis_size("pcol")
    p = lax.axis_index("prow")
    q = lax.axis_index("pcol")
    width = inverse_region.shape[1]
    caps = (BLOCKS, BLOCKS)
    here = jnp.stack([p, q]).astype(jnp.int32)
    core = lax.rem(q, CORES).reshape(1)

    def own_rows(panel):
        return lax.dynamic_slice_in_dim(panel.reshape(-1, width, width), p * ROWS, ROWS, 1)

    mine = jnp.concatenate([own_rows(panel_one), own_rows(panel_two)], axis=0)
    gathered = lax.all_gather(mine, "pcol", axis=0, tiled=True)
    send, own, lists = pick(caps, here, pattern_one, pattern_two, gathered, rows_grid)
    transpose = [
        (a * cols_grid + b, b * cols_grid + a) for a in range(rows_grid) for b in range(cols_grid)
    ]
    rows = lax.ppermute(own, ("prow", "pcol"), transpose)
    panel = swap_axes(send, "prow")
    turned_one, turned_two = turn(caps, lists, inverse_region)
    panel, rows = lax.optimization_barrier((panel, rows))
    keep, give = product(caps, lists, core, turned_one, turned_two, panel)
    got = lax.ppermute(give, "pcol", [(i, i ^ 1) for i in range(cols_grid)])
    paired = (keep + got.astype(F32)).astype(BF16)
    lines = [[z * CORES + c for z in range(CHIPS)] for c in range(CORES)]
    parts = swap_axes(paired, "pcol", lines)
    column_one, column_two, sums = columns(caps, lists, parts, rows, link_block)
    sums = sum_everywhere(sums, rows_grid, cols_grid)
    diagonal_one, cross_two, diagonal_two = diagonals(sums, link_block, inv_diag_one, inv_diag_two)
    return (column_one, diagonal_one, column_two, cross_two, diagonal_two)


def solution(mesh):
    return jax.shard_map(
        shards,
        mesh=mesh,
        in_specs=(P(None, "prow", None, "pcol"), P("pcol", None), P("pcol", None), P(), P(), P(), P(), P()),
        out_specs=(P(None, ("prow", "pcol"), None), P(), P(None, ("prow", "pcol"), None), P(), P()),
        check_vma=False,
    )
```

```python
import functools

import jax
import jax.numpy as jnp
from jax import lax
from jax.experimental import pallas as pl
from jax.experimental.pallas import tpu as pltpu
from jax.sharding import PartitionSpec as P

BF16 = jnp.bfloat16
F32 = jnp.float32
VMEM = pl.BlockSpec(memory_space=pltpu.VMEM)
SMEM = pl.BlockSpec(memory_space=pltpu.SMEM)
HBM = pl.BlockSpec(memory_space=pltpu.HBM)
ANY = pl.BlockSpec(memory_space=pl.ANY)
CHIPS = 8
CORES = 2
ROWS = 16
LANES = 128


def params(mebibytes=16):
    return pltpu.CompilerParams(vmem_limit_bytes=mebibytes * 1024 * 1024)


BLOCKS = 8


def places(block_ids, pattern_one, pattern_two):
    found = []
    for pattern in (pattern_one, pattern_two):
        hits = block_ids[:, None] == pattern[None, :]
        at = jnp.arange(pattern.shape[0], dtype=jnp.int32)[None, :] + 1
        found.append(jnp.sum(jnp.where(hits, at, 0), axis=1) - 1)
    return jnp.concatenate(found)


LIST = 4 * BLOCKS + 1


def compact(found_ref, list_ref):
    for i in range(2 * BLOCKS):
        list_ref[i] = -1
    count = jnp.int32(0)
    for code in range(2 * BLOCKS):
        present = found_ref[code] >= 0
        list_ref[jnp.where(present, count, LIST - 1)] = code
        list_ref[2 * BLOCKS + code] = jnp.where(present, count, -1)
        count = count + present.astype(jnp.int32)


SIDE = 4
FEW = 12


def source(code, s, each):
    one = lax.div(s, each[0]) * sum(each) + lax.rem(s, each[0])
    two = lax.div(s, each[1]) * sum(each) + each[0] + lax.rem(s, each[1])
    return jnp.where(code < BLOCKS, one, two)


def pick_kernel(each, found_ref, gathered_ref, own_ref, low_ref, high_ref, list_ref):
    compact(found_ref, list_ref)
    half = low_ref.shape[0]
    for slot in range(own_ref.shape[0]):
        code = list_ref[slot]
        s = jnp.maximum(found_ref[jnp.maximum(code, 0)], 0)
        block = gathered_ref[source(code, s, each)]
        block = jnp.where(code >= 0, block, jnp.zeros_like(block))
        own_ref[slot] = block
        if slot < half:
            low_ref[slot] = block
        else:
            high_ref[slot - half] = block


def pick(slots, each, found, gathered):
    tail = gathered.shape[1:]
    half = jax.ShapeDtypeStruct((slots // 2,) + tail, BF16)
    return pl.pallas_call(
        functools.partial(pick_kernel, each),
        out_shape=(
            jax.ShapeDtypeStruct((slots,) + tail, BF16), half, half,
            jax.ShapeDtypeStruct((LIST,), jnp.int32),
        ),
        in_specs=[SMEM, VMEM],
        out_specs=(VMEM, VMEM, VMEM, SMEM),
        compiler_params=params(),
        name="pick",
    )(found, gathered)


def product_kernel(rows_ref, cols_ref, here_ref, region_ref, *refs):
    low_refs, high_refs = refs[:SIDE], refs[SIDE:2 * SIDE]
    keep_ref, send_ref, list_ref, region, wide, turned, narrow, panel, total, region_sem, sem = refs[2 * SIDE:]
    width = region.shape[1]
    slots = narrow.shape[0]
    half = slots // 2
    core, depth, x, y = here_ref[0], here_ref[1], here_ref[2], here_ref[3]
    compact(rows_ref, list_ref)

    def region_copy(at):
        return pltpu.make_async_copy(region_ref.at[at], region.at[at], region_sem.at[at])

    def slot_of(code):
        slot = list_ref[2 * BLOCKS + code]
        return slot, (slot >= 0) & (slot < slots)

    copies = []
    for i, (low, high) in enumerate(zip(low_refs, high_refs)):
        for j in range(SIDE):
            for side, ref in enumerate((low, high)):
                dx, dy = (j, i) if side == 0 else (i, j)
                row = lax.rem(y + SIDE - dy, SIDE) * SIDE + lax.rem(x + SIDE - dx, SIDE)
                place = pl.ds(pl.multiple_of(row * ROWS, ROWS), ROWS)
                copies.append(pltpu.make_async_copy(
                    ref.at[j], narrow.at[pl.ds(side * half, half), place, :], sem.at[len(copies)]
                ))
    for copy in copies:
        copy.start()
    for at in range(BLOCKS):
        pl.when(slot_of(at)[1])(region_copy(at).start)
    panel[...] = jnp.zeros(panel.shape, BF16)
    for slot in range(slots):
        @pl.when(list_ref[slot] < 0)
        def _():
            keep_ref[:, slot] = jnp.zeros((CHIPS, ROWS, width), F32)
            send_ref[:, slot] = jnp.zeros((CHIPS, ROWS, width), BF16)

    for copy in copies:
        copy.wait()
    for slot in range(slots):
        code = cols_ref[slot]

        @pl.when(code >= 0)
        def _():
            panel[pl.ds(pl.multiple_of(code * width, width), width), :] = narrow[slot]

    deep = BLOCKS * width

    def multiply(group, slot):
        sums = jnp.dot(turned[...], panel[group * deep:(group + 1) * deep], preferred_element_type=F32)
        total[...] = sums.reshape(total.shape)
        for d in range(CHIPS):
            z = lax.rem(depth + d, CHIPS)
            keep_ref[d, slot] = total[z, core]
            send_ref[d, slot] = total[z, 1 - core].astype(BF16)

    def step(at, carry):
        first, present = slot_of(at)
        second, both = slot_of(BLOCKS + at)

        @pl.when(present)
        def _():
            region_copy(at).wait()
            for h in range(width // LANES):
                part = region[at, :, :, pl.ds(h * LANES, LANES)]
                wide[h] = part.reshape(width * BLOCKS, LANES).astype(F32)
            for c in range(BLOCKS):
                for h in range(width // LANES):
                    turned[:, pl.ds(c * width + h * LANES, LANES)] = wide[
                        h, pl.ds(c, width, stride=BLOCKS), :
                    ].astype(BF16)
            multiply(0, first)
            pl.when(both)(lambda: multiply(1, second))

        return carry

    lax.fori_loop(0, BLOCKS, step, 0)


def product(slots, rows, cols, here, region, lows, highs):
    blocks, width = region.shape[:2]
    shape = (CHIPS, slots, ROWS, width)
    return pl.pallas_call(
        product_kernel,
        out_shape=(
            jax.ShapeDtypeStruct(shape, F32), jax.ShapeDtypeStruct(shape, BF16),
            jax.ShapeDtypeStruct((LIST,), jnp.int32),
        ),
        in_specs=[SMEM, SMEM, SMEM, HBM] + [ANY] * (2 * SIDE),
        out_specs=(VMEM, VMEM, SMEM),
        scratch_shapes=[
            pltpu.VMEM((blocks, width, blocks, width), BF16),
            pltpu.VMEM((width // LANES, width * blocks, LANES), F32),
            pltpu.VMEM((width, blocks * width), BF16),
            pltpu.VMEM((slots, width, width), BF16),
            pltpu.VMEM((2 * blocks * width, width), BF16),
            pltpu.VMEM((CHIPS, CORES, ROWS, width), F32),
            pltpu.SemaphoreType.DMA((blocks,)),
            pltpu.SemaphoreType.DMA((2 * SIDE * SIDE,)),
        ],
        compiler_params=params(48),
        name="product",
    )(rows, cols, here, region, *lows, *highs)


def pair_kernel(keep_ref, got_ref, *out_refs):
    for d, out_ref in enumerate(out_refs):
        out_ref[...] = (keep_ref[d] + got_ref[d].astype(F32)).astype(BF16)


def pair(keep, got):
    share = jax.ShapeDtypeStruct(keep.shape[1:], BF16)
    return pl.pallas_call(
        pair_kernel,
        out_shape=(share,) * CHIPS,
        in_specs=[VMEM, VMEM],
        out_specs=(VMEM,) * CHIPS,
        compiler_params=params(),
        name="pair",
    )(keep, got)


def across(a, b):
    return lax.dot_general(a, b, (((0,), (0,)), ((), ())), preferred_element_type=F32)


def columns_kernel(list_ref, found_ref, rows_ref, link_ref, *refs):
    parts = refs[:CHIPS]
    one_ref, two_ref, sums_ref, sums, rows = refs[CHIPS:]
    blocks, share, width = one_ref.shape
    deep = blocks * share
    rows[...] = jnp.zeros(rows.shape, BF16)
    sums[...] = jnp.zeros(sums.shape, F32)
    for slot in range(parts[0].shape[0]):
        code = list_ref[slot]

        @pl.when(code >= 0)
        def _():
            total = parts[0][slot].astype(F32)
            for part in parts[1:]:
                total = total + part[slot].astype(F32)
            place = pl.ds(pl.multiple_of(code * share, share), share)
            sums[place] = -total
            rows[place] = rows_ref[slot]

    one = sums[:deep].astype(BF16)
    one_ref[...] = one.reshape(one_ref.shape)
    linked = jnp.dot(one, link_ref[...], preferred_element_type=F32)
    second = sums[deep:] - linked
    for at in range(blocks):
        part = slice(at * share, (at + 1) * share)
        kept = jnp.where(found_ref[BLOCKS + at] >= 0, second[part], 0.0)
        two_ref[at] = kept.astype(BF16)
    two = two_ref[...].reshape(deep, width)
    kind = sums_ref.dtype
    sums_ref[:width] = across(rows[:deep], one).astype(kind)
    sums_ref[width:2 * width] = across(one, rows[deep:]).astype(kind)
    sums_ref[2 * width:] = across(rows[deep:], two).astype(kind)


def columns(row_list, found, parts, rows, link):
    share, width = parts[0].shape[1:]
    column = jax.ShapeDtypeStruct((BLOCKS, share, width), BF16)
    return pl.pallas_call(
        columns_kernel,
        out_shape=(column, column, jax.ShapeDtypeStruct((3 * width, width), BF16)),
        in_specs=[SMEM, SMEM, VMEM, VMEM] + [VMEM] * CHIPS,
        out_specs=(VMEM, VMEM, VMEM),
        scratch_shapes=[
            pltpu.VMEM((2 * BLOCKS * share, width), F32),
            pltpu.VMEM((2 * BLOCKS * share, width), BF16),
        ],
        compiler_params=params(),
        name="columns",
    )(row_list, found, rows, link, *parts)


def times_link(value, link, dims):
    total = None
    for _ in range(3):
        part = value.astype(BF16)
        value = value - part.astype(F32)
        term = lax.dot_general(part, link, (dims, ((), ())), preferred_element_type=F32)
        total = term if total is None else total + term
    return total


def diagonals_kernel(sums_ref, link_ref, inv_one_ref, inv_two_ref, one_ref, cross_ref, two_ref):
    width = link_ref.shape[0]
    link = link_ref[...]
    one = inv_one_ref[...] - sums_ref[:width].astype(F32)
    one_ref[...] = one
    cross = -times_link(one, link, ((1,), (0,))) - sums_ref[width:2 * width].astype(F32)
    cross_ref[...] = cross
    two = inv_two_ref[...] - sums_ref[2 * width:].astype(F32)
    two_ref[...] = two - times_link(cross, link, ((0,), (0,))).T


def diagonals(sums, link, inv_one, inv_two):
    square = jax.ShapeDtypeStruct(inv_one.shape, F32)
    return pl.pallas_call(
        diagonals_kernel,
        out_shape=(square, square, square),
        in_specs=[VMEM] * 4,
        out_specs=(VMEM,) * 3,
        compiler_params=params(),
        name="diagonals",
    )(sums, link, inv_one, inv_two)


def swap_axes(value, axes, groups=None):
    return lax.all_to_all(value, axes, 0, 0, axis_index_groups=groups, tiled=True)


def sum_everywhere(sums, rows_grid, cols_grid):
    both = ("prow", "pcol")
    planes = [
        [p * cols_grid + z * CORES + c for p in range(rows_grid) for c in range(CORES)]
        for z in range(CHIPS)
    ]
    lines = [[z * CORES + c for z in range(CHIPS)] for c in range(CORES)]
    ways = rows_grid * CORES
    height, width = sums.shape
    share = height // ways
    pieces = swap_axes(sums.reshape(ways, share, width), both, planes)
    piece = jnp.sum(pieces.astype(F32), axis=0)
    pieces = swap_axes(jnp.broadcast_to(piece, (CHIPS, share, width)), "pcol", lines)
    piece = jnp.sum(pieces, axis=0).astype(BF16)
    pieces = swap_axes(jnp.broadcast_to(piece, (ways, share, width)), both, planes)
    return pieces.reshape(height, width)


def along_z(d):
    lines = [(z, c) for z in range(CHIPS) for c in range(CORES)]
    return [(z * CORES + c, (z + d) % CHIPS * CORES + c) for z, c in lines]


def along_plane(dy, dx):
    places = [(y, x) for y in range(SIDE) for x in range(SIDE)]
    return [(y * SIDE + x, (y + dy) % SIDE * SIDE + (x + dx) % SIDE) for y, x in places]


def spread_plane(low, high):
    hops = (1, SIDE - 1) + tuple(range(2, SIDE - 1))

    def around(value, turn):
        moved = {0: value}
        for d in hops:
            moved[d] = lax.ppermute(value, "prow", turn(d))
        return [moved[d] for d in range(SIDE)]

    def by_x(d):
        return along_plane(0, d)

    def by_y(d):
        return along_plane(d, 0)

    lows, highs = around(low, by_x), around(high, by_y)
    lows, highs = jnp.stack(lows), jnp.stack(highs)
    return around(lows, by_y), around(highs, by_x)


def shards(
    inverse_region, panel_one, panel_two, link_block, inv_diag_one, inv_diag_two,
    pattern_one, pattern_two,
):
    rows_grid = lax.axis_size("prow")
    cols_grid = lax.axis_size("pcol")
    p = lax.axis_index("prow")
    q = lax.axis_index("pcol")
    width = inverse_region.shape[1]
    here = jnp.stack([lax.rem(q, CORES), lax.div(q, CORES), lax.rem(p, SIDE), lax.div(p, SIDE)])
    steps = jnp.arange(BLOCKS, dtype=jnp.int32)
    panels = [panel.reshape(-1, width, width) for panel in (panel_one, panel_two)]
    each = tuple(panel.shape[0] for panel in panels)
    found_cols = places(steps * cols_grid + q, pattern_one, pattern_two)
    found_rows = places(steps * rows_grid + p, pattern_one, pattern_two)
    mine = jnp.concatenate(
        [lax.dynamic_slice_in_dim(panel, p * ROWS, ROWS, 1) for panel in panels], axis=0
    )
    gathered = lax.all_gather(mine, "pcol", axis=0, tiled=True)

    def invert(slots, gathered, found_cols, found_rows, region, link, inv_one, inv_two):
        own, low, high, col_list = pick(slots, each, found_cols, gathered)
        transpose = [
            (a * cols_grid + b, b * cols_grid + a) for a in range(rows_grid) for b in range(cols_grid)
        ]
        rows = lax.ppermute(own, ("prow", "pcol"), transpose)
        lows, highs = spread_plane(low, high)
        keep, give, row_list = product(slots, found_rows, col_list, here, region, lows, highs)
        got = lax.ppermute(give, "pcol", [(i, i ^ 1) for i in range(cols_grid)])
        shares = pair(keep, got)
        parts = [shares[0]]
        for d in (1, 7, 2, 6, 3, 5, 4):
            parts.append(lax.ppermute(shares[d], "pcol", along_z(d)))
        column_one, column_two, sums = columns(row_list, found_rows, parts, rows, link)
        sums = sum_everywhere(sums, rows_grid, cols_grid)
        diagonal_one, cross_two, diagonal_two = diagonals(sums, link, inv_one, inv_two)
        return (column_one, diagonal_one, column_two, cross_two, diagonal_two)

    classes = jnp.arange(rows_grid, dtype=jnp.int32)[:, None]
    members = sum(
        jnp.sum((lax.rem(pattern, rows_grid)[None, :] == classes).astype(jnp.int32), axis=1)
        for pattern in (pattern_one, pattern_two)
    )
    fits = jnp.all(members <= FEW)
    given = (gathered, found_cols, found_rows, inverse_region, link_block, inv_diag_one, inv_diag_two)
    return lax.cond(
        fits,
        lambda outs, *given: outs,
        lambda outs, *given: invert(2 * BLOCKS, *given),
        invert(FEW, *given), *given,
    )


def solution(mesh):
    return jax.shard_map(
        shards,
        mesh=mesh,
        in_specs=(P(None, "prow", None, "pcol"), P("pcol", None), P("pcol", None), P(), P(), P(), P(), P()),
        out_specs=(P(None, ("prow", "pcol"), None), P(), P(None, ("prow", "pcol"), None), P(), P()),
        check_vma=False,
    )
```

```python
import functools

import jax
import jax.numpy as jnp
from jax import lax
from jax.experimental import pallas as pl
from jax.experimental.pallas import tpu as pltpu
from jax.sharding import PartitionSpec as P

BF16 = jnp.bfloat16
F32 = jnp.float32
VMEM = pl.BlockSpec(memory_space=pltpu.VMEM)
SMEM = pl.BlockSpec(memory_space=pltpu.SMEM)
HBM = pl.BlockSpec(memory_space=pltpu.HBM)
CHIPS = 8
CORES = 2
ROWS = 16
LANES = 128


def params(mebibytes=16):
    return pltpu.CompilerParams(vmem_limit_bytes=mebibytes * 1024 * 1024)


BLOCKS = 8


def places(block_ids, pattern_one, pattern_two):
    found = []
    for pattern in (pattern_one, pattern_two):
        hits = block_ids[:, None] == pattern[None, :]
        at = jnp.arange(pattern.shape[0], dtype=jnp.int32)[None, :] + 1
        found.append(jnp.sum(jnp.where(hits, at, 0), axis=1) - 1)
    return jnp.concatenate(found)


LIST = 4 * BLOCKS + 1


def compact(found_ref, list_ref):
    for i in range(2 * BLOCKS):
        list_ref[i] = -1
    count = jnp.int32(0)
    for code in range(2 * BLOCKS):
        present = found_ref[code] >= 0
        list_ref[jnp.where(present, count, LIST - 1)] = code
        list_ref[2 * BLOCKS + code] = jnp.where(present, count, -1)
        count = count + present.astype(jnp.int32)


SIDE = 4
FEW = 12


def source(code, s, each):
    one = lax.div(s, each[0]) * sum(each) + lax.rem(s, each[0])
    two = lax.div(s, each[1]) * sum(each) + each[0] + lax.rem(s, each[1])
    return jnp.where(code < BLOCKS, one, two)


def pick_kernel(each, found_ref, other_ref, gathered_ref, other_out_ref, low_ref, high_ref, list_ref, other_list):
    half = low_ref.shape[0]

    def chosen(found, codes, slot):
        code = codes[slot]
        s = jnp.maximum(found[jnp.maximum(code, 0)], 0)
        block = gathered_ref[source(code, s, each)]
        return jnp.where(code >= 0, block, jnp.zeros_like(block))

    compact(found_ref, list_ref)
    compact(other_ref, other_list)
    for slot in range(2 * half):
        block = chosen(found_ref, list_ref, slot)
        if slot < half:
            low_ref[slot] = block
        else:
            high_ref[slot - half] = block
        other_out_ref[slot] = chosen(other_ref, other_list, slot)


def pick(slots, each, found, other, gathered):
    tail = gathered.shape[1:]
    half = jax.ShapeDtypeStruct((slots // 2,) + tail, BF16)
    return pl.pallas_call(
        functools.partial(pick_kernel, each),
        out_shape=(
            jax.ShapeDtypeStruct((slots,) + tail, BF16), half, half,
            jax.ShapeDtypeStruct((LIST,), jnp.int32),
        ),
        in_specs=[SMEM, SMEM, VMEM],
        out_specs=(VMEM, VMEM, VMEM, SMEM),
        scratch_shapes=[pltpu.SMEM((LIST,), jnp.int32)],
        compiler_params=params(),
        name="pick",
    )(found, other, gathered)


def product_kernel(rows_ref, cols_ref, here_ref, region_ref, *refs):
    low_refs, high_refs = refs[:SIDE], refs[SIDE:2 * SIDE]
    keep_ref, send_ref, list_ref, region, wide, turned, panel, total, region_sem = refs[2 * SIDE:]
    width = region.shape[1]
    slots = keep_ref.shape[1]
    half = slots // 2
    core, depth, x, y = here_ref[0], here_ref[1], here_ref[2], here_ref[3]
    compact(rows_ref, list_ref)

    def region_copy(at):
        return pltpu.make_async_copy(region_ref.at[at], region.at[at], region_sem.at[at])

    def slot_of(code):
        slot = list_ref[2 * BLOCKS + code]
        return slot, (slot >= 0) & (slot < slots)

    for at in range(BLOCKS):
        pl.when(slot_of(at)[1])(region_copy(at).start)
    panel[...] = jnp.zeros(panel.shape, BF16)
    for slot in range(slots):
        @pl.when(list_ref[slot] < 0)
        def _():
            keep_ref[:, slot] = jnp.zeros((CHIPS, ROWS, width), F32)
            send_ref[:, slot] = jnp.zeros((CHIPS, ROWS, width), BF16)

    rows = [[[None, None] for _ in range(SIDE)] for _ in range(SIDE)]
    for i in range(SIDE):
        for j in range(SIDE):
            for side, (dx, dy) in enumerate(((j, i), (i, j))):
                row = lax.rem(y + SIDE - dy, SIDE) * SIDE + lax.rem(x + SIDE - dx, SIDE)
                rows[i][j][side] = row * ROWS
    for slot in range(slots):
        code = cols_ref[slot]
        side, local = divmod(slot, half)
        refs_here = (low_refs, high_refs)[side]

        @pl.when(code >= 0)
        def _():
            for i in range(SIDE):
                for j in range(SIDE):
                    place = pl.multiple_of(code * width + rows[i][j][side], ROWS)
                    panel[pl.ds(place, ROWS), :] = refs_here[i][j, local]

    deep = BLOCKS * width

    def multiply(group, slot):
        sums = jnp.dot(turned[...], panel[group * deep:(group + 1) * deep], preferred_element_type=F32)
        total[...] = sums.reshape(total.shape)
        for d in range(CHIPS):
            z = lax.rem(depth + d, CHIPS)
            keep_ref[d, slot] = total[z, core]
            send_ref[d, slot] = total[z, 1 - core].astype(BF16)

    def step(at, carry):
        first, present = slot_of(at)
        second, both = slot_of(BLOCKS + at)

        @pl.when(present)
        def _():
            region_copy(at).wait()
            for h in range(width // LANES):
                part = region[at, :, :, pl.ds(h * LANES, LANES)]
                wide[h] = part.reshape(width * BLOCKS, LANES).astype(F32)
            for c in range(BLOCKS):
                for h in range(width // LANES):
                    turned[:, pl.ds(c * width + h * LANES, LANES)] = wide[
                        h, pl.ds(c, width, stride=BLOCKS), :
                    ].astype(BF16)
            multiply(0, first)
            pl.when(both)(lambda: multiply(1, second))

        return carry

    lax.fori_loop(0, BLOCKS, step, 0)


def product(slots, rows, cols, here, region, lows, highs):
    blocks, width = region.shape[:2]
    shape = (CHIPS, slots, ROWS, width)
    return pl.pallas_call(
        product_kernel,
        out_shape=(
            jax.ShapeDtypeStruct(shape, F32), jax.ShapeDtypeStruct(shape, BF16),
            jax.ShapeDtypeStruct((LIST,), jnp.int32),
        ),
        in_specs=[SMEM, SMEM, SMEM, HBM] + [VMEM] * (2 * SIDE),
        out_specs=(VMEM, VMEM, SMEM),
        scratch_shapes=[
            pltpu.VMEM((blocks, width, blocks, width), BF16),
            pltpu.VMEM((width // LANES, width * blocks, LANES), F32),
            pltpu.VMEM((width, blocks * width), BF16),
            pltpu.VMEM((2 * blocks * width, width), BF16),
            pltpu.VMEM((CHIPS, CORES, ROWS, width), F32),
            pltpu.SemaphoreType.DMA((blocks,)),
        ],
        compiler_params=params(48),
        cost_estimate=pl.CostEstimate(
            flops=2 * slots * blocks * width**3, bytes_accessed=2 * region.size, transcendentals=0
        ),
        name="product",
    )(rows, cols, here, region, *lows, *highs)


UP = (3, 1)
DOWN = (4, 6)
ON = (2, 5, 7)


def pair_kernel(keep_ref, got_ref, own_ref, up_ref, down_ref, on_ref):
    def share(d):
        return keep_ref[d] + got_ref[d].astype(F32)

    own_ref[...] = share(0)
    for out_ref, ways in ((up_ref, UP), (down_ref, DOWN), (on_ref, ON)):
        for i, d in enumerate(ways):
            out_ref[i] = share(d).astype(out_ref.dtype)


def pair(keep, got):
    share = keep.shape[1:]
    return pl.pallas_call(
        pair_kernel,
        out_shape=(
            jax.ShapeDtypeStruct(share, F32),
            jax.ShapeDtypeStruct((len(UP),) + share, BF16),
            jax.ShapeDtypeStruct((len(DOWN),) + share, BF16),
            jax.ShapeDtypeStruct((len(ON),) + share, F32),
        ),
        in_specs=[VMEM, VMEM],
        out_specs=(VMEM,) * 4,
        compiler_params=params(),
        name="pair",
    )(keep, got)


def merge_kernel(on_ref, up_ref, down_ref, *out_refs):
    for i, (out_ref, came) in enumerate(zip(out_refs, (up_ref.at[0], down_ref.at[0], down_ref.at[1]))):
        out_ref[...] = (on_ref[i] + came[...].astype(F32)).astype(BF16)


def merge(on, up, down):
    share = jax.ShapeDtypeStruct(on.shape[1:], BF16)
    return pl.pallas_call(
        merge_kernel,
        out_shape=(share,) * len(ON),
        in_specs=[VMEM] * 3,
        out_specs=(VMEM,) * len(ON),
        compiler_params=params(),
        name="merge",
    )(on, up, down)


def sum_along_z(keep, got):
    own, up, down, on = pair(keep, got)
    up = lax.ppermute(up, "pcol", along_z(1))
    down = lax.ppermute(down, "pcol", along_z(CHIPS - 1))
    on = merge(on, up, down)
    came = [lax.ppermute(on[i], "pcol", along_z(ON[i])) for i in (1, 2, 0)]
    return [own, up] + came


def across(a, b):
    return lax.dot_general(a, b, (((0,), (0,)), ((), ())), preferred_element_type=F32)


def columns_kernel(list_ref, found_ref, rows_ref, link_ref, *refs):
    own_ref, up_ref = refs[:2]
    came_refs = refs[2:2 + len(ON)]
    one_ref, two_ref, sums_ref, sums, rows = refs[2 + len(ON):]
    blocks, share, width = one_ref.shape
    deep = blocks * share
    rows[...] = jnp.zeros(rows.shape, BF16)
    sums[...] = jnp.zeros(sums.shape, F32)
    for slot in range(own_ref.shape[0]):
        code = list_ref[slot]

        @pl.when(code >= 0)
        def _():
            total = own_ref[slot] + up_ref[1, slot].astype(F32)
            for came in came_refs:
                total = total + came[slot].astype(F32)
            place = pl.ds(pl.multiple_of(code * share, share), share)
            sums[place] = -total
            rows[place] = rows_ref[slot]

    one = sums[:deep].astype(BF16)
    one_ref[...] = one.reshape(one_ref.shape)
    linked = jnp.dot(one, link_ref[...], preferred_element_type=F32)
    second = sums[deep:] - linked
    for at in range(blocks):
        part = slice(at * share, (at + 1) * share)
        kept = jnp.where(found_ref[BLOCKS + at] >= 0, second[part], 0.0)
        two_ref[at] = kept.astype(BF16)
    two = two_ref[...].reshape(deep, width)
    kind = sums_ref.dtype
    sums_ref[:width] = across(rows[:deep], one).astype(kind)
    sums_ref[width:2 * width] = across(one, rows[deep:]).astype(kind)
    sums_ref[2 * width:] = across(rows[deep:], two).astype(kind)


def columns(row_list, found, parts, rows, link):
    share, width = parts[0].shape[1:]
    column = jax.ShapeDtypeStruct((BLOCKS, share, width), BF16)
    return pl.pallas_call(
        columns_kernel,
        out_shape=(column, column, jax.ShapeDtypeStruct((3 * width, width), BF16)),
        in_specs=[SMEM, SMEM, VMEM, VMEM] + [VMEM] * (2 + len(ON)),
        out_specs=(VMEM, VMEM, VMEM),
        scratch_shapes=[
            pltpu.VMEM((2 * BLOCKS * share, width), F32),
            pltpu.VMEM((2 * BLOCKS * share, width), BF16),
        ],
        compiler_params=params(),
        name="columns",
    )(row_list, found, rows, link, *parts)


def times_link(value, link, dims):
    total = None
    for _ in range(3):
        part = value.astype(BF16)
        value = value - part.astype(F32)
        term = lax.dot_general(part, link, (dims, ((), ())), preferred_element_type=F32)
        total = term if total is None else total + term
    return total


def diagonals_kernel(sums_ref, link_ref, inv_one_ref, inv_two_ref, one_ref, cross_ref, two_ref):
    width = link_ref.shape[0]
    link = link_ref[...]
    one = inv_one_ref[...] - sums_ref[:width].astype(F32)
    one_ref[...] = one
    cross = -times_link(one, link, ((1,), (0,))) - sums_ref[width:2 * width].astype(F32)
    cross_ref[...] = cross
    two = inv_two_ref[...] - sums_ref[2 * width:].astype(F32)
    two_ref[...] = two - times_link(cross, link, ((0,), (0,))).T


def diagonals(sums, link, inv_one, inv_two):
    square = jax.ShapeDtypeStruct(inv_one.shape, F32)
    return pl.pallas_call(
        diagonals_kernel,
        out_shape=(square, square, square),
        in_specs=[VMEM] * 4,
        out_specs=(VMEM,) * 3,
        compiler_params=params(),
        name="diagonals",
    )(sums, link, inv_one, inv_two)


def swap_axes(value, axes, groups=None):
    return lax.all_to_all(value, axes, 0, 0, axis_index_groups=groups, tiled=True)


def sum_everywhere(sums, rows_grid, cols_grid):
    both = ("prow", "pcol")
    planes = [
        [p * cols_grid + z * CORES + c for p in range(rows_grid) for c in range(CORES)]
        for z in range(CHIPS)
    ]
    ways = rows_grid * CORES
    height, width = sums.shape
    share = height // ways
    pieces = swap_axes(sums.reshape(ways, share, width), both, planes)
    piece = jnp.sum(pieces.astype(F32), axis=0)
    lines = [[z * CORES + c for z in range(CHIPS)] for c in range(CORES)]
    pieces = swap_axes(jnp.broadcast_to(piece, (CHIPS, share, width)), "pcol", lines)
    piece = jnp.sum(pieces, axis=0).astype(BF16)
    pieces = swap_axes(jnp.broadcast_to(piece, (ways, share, width)), both, planes)
    return pieces.reshape(height, width)


def along_z(d):
    lines = [(z, c) for z in range(CHIPS) for c in range(CORES)]
    return [(z * CORES + c, (z + d) % CHIPS * CORES + c) for z, c in lines]


def along_plane(dy, dx):
    places = [(y, x) for y in range(SIDE) for x in range(SIDE)]
    return [(y * SIDE + x, (y + dy) % SIDE * SIDE + (x + dx) % SIDE) for y, x in places]


def spread_plane(low, high):
    hops = (1, SIDE - 1) + tuple(range(2, SIDE - 1))

    def around(value, turn):
        moved = {0: value}
        for d in hops:
            moved[d] = lax.ppermute(value, "prow", turn(d))
        return [moved[d] for d in range(SIDE)]

    def by_x(d):
        return along_plane(0, d)

    def by_y(d):
        return along_plane(d, 0)

    lows, highs = around(low, by_x), around(high, by_y)
    lows, highs = jnp.stack(lows), jnp.stack(highs)
    return around(lows, by_y), around(highs, by_x)


def shards(
    inverse_region, panel_one, panel_two, link_block, inv_diag_one, inv_diag_two,
    pattern_one, pattern_two,
):
    rows_grid = lax.axis_size("prow")
    cols_grid = lax.axis_size("pcol")
    p = lax.axis_index("prow")
    q = lax.axis_index("pcol")
    width = inverse_region.shape[1]
    here = jnp.stack([lax.rem(q, CORES), lax.div(q, CORES), lax.rem(p, SIDE), lax.div(p, SIDE)])
    steps = jnp.arange(BLOCKS, dtype=jnp.int32)
    panels = [panel.reshape(-1, width, width) for panel in (panel_one, panel_two)]
    each = tuple(panel.shape[0] for panel in panels)
    found_cols = places(steps * cols_grid + q, pattern_one, pattern_two)
    found_rows = places(steps * rows_grid + p, pattern_one, pattern_two)
    found_other = places(steps * rows_grid + (q - p) % rows_grid, pattern_one, pattern_two)
    mine = jnp.concatenate(
        [lax.dynamic_slice_in_dim(panel, p * ROWS, ROWS, 1) for panel in panels], axis=0
    )
    gathered = lax.all_gather(mine, "pcol", axis=0, tiled=True)

    def invert(slots, gathered, found_cols, found_other, found_rows, region, link, inv_one, inv_two):
        other, low, high, col_list = pick(slots, each, found_cols, found_other, gathered)
        moves = [
            (a * cols_grid + b, (b - a) % rows_grid * cols_grid + a)
            for a in range(rows_grid) for b in range(cols_grid)
        ]
        rows = lax.ppermute(other, ("prow", "pcol"), moves)
        lows, highs = spread_plane(low, high)
        keep, give, row_list = product(slots, found_rows, col_list, here, region, lows, highs)
        give, rows = lax.optimization_barrier((give, rows))
        got = lax.ppermute(give, "pcol", [(i, i ^ 1) for i in range(cols_grid)])
        parts = sum_along_z(keep, got)
        column_one, column_two, sums = columns(row_list, found_rows, parts, rows, link)
        sums = sum_everywhere(sums, rows_grid, cols_grid)
        diagonal_one, cross_two, diagonal_two = diagonals(sums, link, inv_one, inv_two)
        return (column_one, diagonal_one, column_two, cross_two, diagonal_two)

    classes = jnp.arange(rows_grid, dtype=jnp.int32)[:, None]
    members = sum(
        jnp.sum((lax.rem(pattern, rows_grid)[None, :] == classes).astype(jnp.int32), axis=1)
        for pattern in (pattern_one, pattern_two)
    )
    fits = jnp.all(members <= FEW)
    given = (gathered, found_cols, found_other, found_rows, inverse_region, link_block, inv_diag_one, inv_diag_two)
    return lax.cond(
        fits,
        lambda outs, *given: outs,
        lambda outs, *given: invert(2 * BLOCKS, *given),
        invert(FEW, *given), *given,
    )


def solution(mesh):
    return jax.shard_map(
        shards,
        mesh=mesh,
        in_specs=(P(None, "prow", None, "pcol"), P("pcol", None), P("pcol", None), P(), P(), P(), P(), P()),
        out_specs=(P(None, ("prow", "pcol"), None), P(), P(None, ("prow", "pcol"), None), P(), P()),
        check_vma=False,
    )
```

```python
import functools

import jax
import jax.numpy as jnp
from jax import lax
from jax.experimental import pallas as pl
from jax.experimental.pallas import tpu as pltpu
from jax.sharding import PartitionSpec as P

BF16 = jnp.bfloat16
F32 = jnp.float32
VMEM = pl.BlockSpec(memory_space=pltpu.VMEM)
SMEM = pl.BlockSpec(memory_space=pltpu.SMEM)
HBM = pl.BlockSpec(memory_space=pltpu.HBM)
CHIPS = 8
CORES = 2
ROWS = 16
LANES = 128


def params(mebibytes=16):
    return pltpu.CompilerParams(vmem_limit_bytes=mebibytes * 1024 * 1024)


BLOCKS = 8


def places(block_ids, pattern_one, pattern_two):
    found = []
    for pattern in (pattern_one, pattern_two):
        hits = block_ids[:, None] == pattern[None, :]
        at = jnp.arange(pattern.shape[0], dtype=jnp.int32)[None, :] + 1
        found.append(jnp.sum(jnp.where(hits, at, 0), axis=1) - 1)
    return jnp.concatenate(found)


LIST = 4 * BLOCKS + 1


def compact(found_ref, list_ref):
    for i in range(2 * BLOCKS):
        list_ref[i] = -1
    count = jnp.int32(0)
    for code in range(2 * BLOCKS):
        present = found_ref[code] >= 0
        list_ref[jnp.where(present, count, LIST - 1)] = code
        list_ref[2 * BLOCKS + code] = jnp.where(present, count, -1)
        count = count + present.astype(jnp.int32)


SIDE = 4
FEW = 12
AHEAD = 3


def source(code, s, each):
    one = lax.div(s, each[0]) * sum(each) + lax.rem(s, each[0])
    two = lax.div(s, each[1]) * sum(each) + each[0] + lax.rem(s, each[1])
    return jnp.where(code < BLOCKS, one, two)


def pick_kernel(each, found_ref, other_ref, gathered_ref, other_out_ref, low_ref, high_ref, list_ref, other_list):
    half = low_ref.shape[0]

    def chosen(found, codes, slot):
        code = codes[slot]
        s = jnp.maximum(found[jnp.maximum(code, 0)], 0)
        block = gathered_ref[source(code, s, each)]
        return jnp.where(code >= 0, block, jnp.zeros_like(block))

    compact(found_ref, list_ref)
    compact(other_ref, other_list)
    for slot in range(2 * half):
        block = chosen(found_ref, list_ref, slot)
        if slot < half:
            low_ref[slot] = block
        else:
            high_ref[slot - half] = block
        other_out_ref[slot] = chosen(other_ref, other_list, slot)


def pick(slots, each, found, other, gathered):
    tail = gathered.shape[1:]
    half = jax.ShapeDtypeStruct((slots // 2,) + tail, BF16)
    return pl.pallas_call(
        functools.partial(pick_kernel, each),
        out_shape=(
            jax.ShapeDtypeStruct((slots,) + tail, BF16), half, half,
            jax.ShapeDtypeStruct((LIST,), jnp.int32),
        ),
        in_specs=[SMEM, SMEM, VMEM],
        out_specs=(VMEM, VMEM, VMEM, SMEM),
        scratch_shapes=[pltpu.SMEM((LIST,), jnp.int32)],
        compiler_params=params(),
        name="pick",
    )(found, other, gathered)


def product_kernel(rows_ref, cols_ref, here_ref, region_ref, *refs):
    low_refs, high_refs = refs[:SIDE], refs[SIDE:2 * SIDE]
    keep_ref, send_ref, list_ref, region, wide, turned, panel, total, region_sem = refs[2 * SIDE:]
    width = region.shape[1]
    slots = keep_ref.shape[1]
    half = slots // 2
    core, depth, x, y = here_ref[0], here_ref[1], here_ref[2], here_ref[3]
    compact(rows_ref, list_ref)

    def region_copy(at):
        return pltpu.make_async_copy(region_ref.at[at], region.at[at], region_sem.at[at])

    def slot_of(code):
        slot = list_ref[2 * BLOCKS + code]
        return slot, (slot >= 0) & (slot < slots)

    def fetch(u):
        at = list_ref[jnp.minimum(u, BLOCKS - 1)]
        pl.when((u < BLOCKS) & (at >= 0) & (at < BLOCKS))(lambda: region_copy(at).start())

    for u in range(AHEAD):
        fetch(u)
    panel[...] = jnp.zeros(panel.shape, BF16)
    for slot in range(slots):
        @pl.when(list_ref[slot] < 0)
        def _():
            keep_ref[:, slot] = jnp.zeros((CHIPS, ROWS, width), F32)
            send_ref[:, slot] = jnp.zeros((CHIPS, ROWS, width), BF16)

    rows = [[[None, None] for _ in range(SIDE)] for _ in range(SIDE)]
    for i in range(SIDE):
        for j in range(SIDE):
            for side, (dx, dy) in enumerate(((j, i), (i, j))):
                row = lax.rem(y + SIDE - dy, SIDE) * SIDE + lax.rem(x + SIDE - dx, SIDE)
                rows[i][j][side] = row * ROWS
    for slot in range(slots):
        code = cols_ref[slot]
        side, local = divmod(slot, half)
        refs_here = (low_refs, high_refs)[side]

        @pl.when(code >= 0)
        def _():
            for i in range(SIDE):
                for j in range(SIDE):
                    place = pl.multiple_of(code * width + rows[i][j][side], ROWS)
                    panel[pl.ds(place, ROWS), :] = refs_here[i][j, local]

    deep = BLOCKS * width

    def multiply(group, slot):
        sums = jnp.dot(turned[...], panel[group * deep:(group + 1) * deep], preferred_element_type=F32)
        total[...] = sums.reshape(total.shape)
        for d in range(CHIPS):
            z = lax.rem(depth + d, CHIPS)
            keep_ref[d, slot] = total[z, core]
            send_ref[d, slot] = total[z, 1 - core].astype(BF16)

    def step(u, carry):
        at = list_ref[u]
        present = (at >= 0) & (at < BLOCKS)
        second, both = slot_of(BLOCKS + jnp.where(present, at, 0))

        @pl.when(present)
        def _():
            fetch(u + AHEAD)
            region_copy(at).wait()
            for h in range(width // LANES):
                part = region[at, :, :, pl.ds(h * LANES, LANES)]
                wide[h] = part.reshape(width * BLOCKS, LANES).astype(F32)
            for c in range(BLOCKS):
                for h in range(width // LANES):
                    turned[:, pl.ds(c * width + h * LANES, LANES)] = wide[
                        h, pl.ds(c, width, stride=BLOCKS), :
                    ].astype(BF16)
            multiply(0, u)
            pl.when(both)(lambda: multiply(1, second))

        return carry

    lax.fori_loop(0, BLOCKS, step, 0)


def product(slots, rows, cols, here, region, lows, highs):
    blocks, width = region.shape[:2]
    shape = (CHIPS, slots, ROWS, width)
    return pl.pallas_call(
        product_kernel,
        out_shape=(
            jax.ShapeDtypeStruct(shape, F32), jax.ShapeDtypeStruct(shape, BF16),
            jax.ShapeDtypeStruct((LIST,), jnp.int32),
        ),
        in_specs=[SMEM, SMEM, SMEM, HBM] + [VMEM] * (2 * SIDE),
        out_specs=(VMEM, VMEM, SMEM),
        scratch_shapes=[
            pltpu.VMEM((blocks, width, blocks, width), BF16),
            pltpu.VMEM((width // LANES, width * blocks, LANES), F32),
            pltpu.VMEM((width, blocks * width), BF16),
            pltpu.VMEM((2 * blocks * width, width), BF16),
            pltpu.VMEM((CHIPS, CORES, ROWS, width), F32),
            pltpu.SemaphoreType.DMA((blocks,)),
        ],
        compiler_params=params(48),
        cost_estimate=pl.CostEstimate(
            flops=2 * slots * blocks * width**3, bytes_accessed=2 * region.size, transcendentals=0
        ),
        name="product",
    )(rows, cols, here, region, *lows, *highs)


UP = (3, 1)
DOWN = (4, 6)
ON = (2, 5, 7)


def pair_kernel(keep_ref, got_ref, own_ref, up_ref, down_ref, on_ref):
    def share(d):
        return keep_ref[d] + got_ref[d].astype(F32)

    own_ref[...] = share(0)
    for out_ref, ways in ((up_ref, UP), (down_ref, DOWN), (on_ref, ON)):
        for i, d in enumerate(ways):
            out_ref[i] = share(d).astype(out_ref.dtype)


def pair(keep, got):
    share = keep.shape[1:]
    return pl.pallas_call(
        pair_kernel,
        out_shape=(
            jax.ShapeDtypeStruct(share, F32),
            jax.ShapeDtypeStruct((len(UP),) + share, BF16),
            jax.ShapeDtypeStruct((len(DOWN),) + share, BF16),
            jax.ShapeDtypeStruct((len(ON),) + share, F32),
        ),
        in_specs=[VMEM, VMEM],
        out_specs=(VMEM,) * 4,
        compiler_params=params(),
        name="pair",
    )(keep, got)


def merge_kernel(on_ref, up_ref, down_ref, *out_refs):
    for i, (out_ref, came) in enumerate(zip(out_refs, (up_ref.at[0], down_ref.at[0], down_ref.at[1]))):
        out_ref[...] = (on_ref[i] + came[...].astype(F32)).astype(BF16)


def merge(on, up, down):
    share = jax.ShapeDtypeStruct(on.shape[1:], BF16)
    return pl.pallas_call(
        merge_kernel,
        out_shape=(share,) * len(ON),
        in_specs=[VMEM] * 3,
        out_specs=(VMEM,) * len(ON),
        compiler_params=params(),
        name="merge",
    )(on, up, down)


def sum_along_z(keep, got, fits):
    own, up, down, on = pair(keep, got)
    up = lax.ppermute(up, "pcol", along_z(1))
    down = lax.ppermute(down, "pcol", along_z(CHIPS - 1))
    up, fits = lax.optimization_barrier((up, fits))
    on = merge(on, up, down)
    came = [lax.ppermute(on[i], "pcol", along_z(ON[i])) for i in (1, 2, 0)]
    return [own, up] + came, fits


def across(a, b):
    return lax.dot_general(a, b, (((0,), (0,)), ((), ())), preferred_element_type=F32)


def columns_kernel(list_ref, found_ref, rows_ref, link_ref, *refs):
    own_ref, up_ref = refs[:2]
    came_refs = refs[2:2 + len(ON)]
    one_ref, two_ref, sums_ref, sums, rows = refs[2 + len(ON):]
    blocks, share, width = one_ref.shape
    deep = blocks * share
    rows[...] = jnp.zeros(rows.shape, BF16)
    sums[...] = jnp.zeros(sums.shape, F32)
    for slot in range(own_ref.shape[0]):
        code = list_ref[slot]

        @pl.when(code >= 0)
        def _():
            total = own_ref[slot] + up_ref[1, slot].astype(F32)
            for came in came_refs:
                total = total + came[slot].astype(F32)
            place = pl.ds(pl.multiple_of(code * share, share), share)
            sums[place] = -total
            rows[place] = rows_ref[slot]

    one = sums[:deep].astype(BF16)
    one_ref[...] = one.reshape(one_ref.shape)
    linked = jnp.dot(one, link_ref[...], preferred_element_type=F32)
    second = sums[deep:] - linked
    for at in range(blocks):
        part = slice(at * share, (at + 1) * share)
        kept = jnp.where(found_ref[BLOCKS + at] >= 0, second[part], 0.0)
        two_ref[at] = kept.astype(BF16)
    two = two_ref[...].reshape(deep, width)
    kind = sums_ref.dtype
    sums_ref[:width] = across(rows[:deep], one).astype(kind)
    sums_ref[width:2 * width] = across(one, rows[deep:]).astype(kind)
    sums_ref[2 * width:] = across(rows[deep:], two).astype(kind)


def columns(row_list, found, parts, rows, link):
    share, width = parts[0].shape[1:]
    column = jax.ShapeDtypeStruct((BLOCKS, share, width), BF16)
    return pl.pallas_call(
        columns_kernel,
        out_shape=(column, column, jax.ShapeDtypeStruct((3 * width, width), BF16)),
        in_specs=[SMEM, SMEM, VMEM, VMEM] + [VMEM] * (2 + len(ON)),
        out_specs=(VMEM, VMEM, VMEM),
        scratch_shapes=[
            pltpu.VMEM((2 * BLOCKS * share, width), F32),
            pltpu.VMEM((2 * BLOCKS * share, width), BF16),
        ],
        compiler_params=params(),
        name="columns",
    )(row_list, found, rows, link, *parts)


def times_link(value, link, dims):
    total = None
    for _ in range(3):
        part = value.astype(BF16)
        value = value - part.astype(F32)
        term = lax.dot_general(part, link, (dims, ((), ())), preferred_element_type=F32)
        total = term if total is None else total + term
    return total


def diagonals_kernel(sums_ref, link_ref, inv_one_ref, inv_two_ref, one_ref, cross_ref, two_ref):
    width = link_ref.shape[0]
    link = link_ref[...]
    one = inv_one_ref[...] - sums_ref[:width].astype(F32)
    one_ref[...] = one
    cross = -times_link(one, link, ((1,), (0,))) - sums_ref[width:2 * width].astype(F32)
    cross_ref[...] = cross
    two = inv_two_ref[...] - sums_ref[2 * width:].astype(F32)
    two_ref[...] = two - times_link(cross, link, ((0,), (0,))).T


def diagonals(sums, link, inv_one, inv_two):
    square = jax.ShapeDtypeStruct(inv_one.shape, F32)
    return pl.pallas_call(
        diagonals_kernel,
        out_shape=(square, square, square),
        in_specs=[VMEM] * 4,
        out_specs=(VMEM,) * 3,
        compiler_params=params(),
        name="diagonals",
    )(sums, link, inv_one, inv_two)


def fold_kernel(pieces_ref, out_ref):
    total = pieces_ref[0].astype(F32)
    for i in range(1, pieces_ref.shape[0]):
        total = total + pieces_ref[i].astype(F32)
    for i in range(out_ref.shape[0]):
        out_ref[i] = total.astype(out_ref.dtype)


def fold(pieces, copies, dtype):
    return pl.pallas_call(
        fold_kernel,
        out_shape=jax.ShapeDtypeStruct((copies,) + pieces.shape[1:], dtype),
        in_specs=[VMEM],
        out_specs=VMEM,
        compiler_params=params(),
        name="fold",
    )(pieces)


def swap_axes(value, axes, groups=None):
    return lax.all_to_all(value, axes, 0, 0, axis_index_groups=groups, tiled=True)


def sum_everywhere(sums, rows_grid, cols_grid):
    both = ("prow", "pcol")
    planes = [
        [p * cols_grid + z * CORES + c for p in range(rows_grid) for c in range(CORES)]
        for z in range(CHIPS)
    ]
    ways = rows_grid * CORES
    height, width = sums.shape
    share = height // ways
    pieces = swap_axes(sums.reshape(ways, share, width), both, planes)
    lines = [[z * CORES + c for z in range(CHIPS)] for c in range(CORES)]
    pieces = swap_axes(fold(pieces, CHIPS, F32), "pcol", lines)
    pieces = swap_axes(fold(pieces, ways, BF16), both, planes)
    return pieces.reshape(height, width)


def along_z(d):
    lines = [(z, c) for z in range(CHIPS) for c in range(CORES)]
    return [(z * CORES + c, (z + d) % CHIPS * CORES + c) for z, c in lines]


def along_plane(dy, dx):
    places = [(y, x) for y in range(SIDE) for x in range(SIDE)]
    return [(y * SIDE + x, (y + dy) % SIDE * SIDE + (x + dx) % SIDE) for y, x in places]


def spread_plane(low, high):
    hops = tuple(range(2, SIDE - 1)) + (1, SIDE - 1)

    def around(value, turn):
        moved = {0: value}
        for d in hops:
            moved[d] = lax.ppermute(value, "prow", turn(d))
        return [moved[d] for d in range(SIDE)]

    def by_x(d):
        return along_plane(0, d)

    def by_y(d):
        return along_plane(d, 0)

    lows, highs = around(low, by_x), around(high, by_y)
    lows, highs = jnp.stack(lows), jnp.stack(highs)
    return around(lows, by_y), around(highs, by_x)


def shards(
    inverse_region, panel_one, panel_two, link_block, inv_diag_one, inv_diag_two,
    pattern_one, pattern_two,
):
    rows_grid = lax.axis_size("prow")
    cols_grid = lax.axis_size("pcol")
    p = lax.axis_index("prow")
    q = lax.axis_index("pcol")
    width = inverse_region.shape[1]
    here = jnp.stack([lax.rem(q, CORES), lax.div(q, CORES), lax.rem(p, SIDE), lax.div(p, SIDE)])
    steps = jnp.arange(BLOCKS, dtype=jnp.int32)
    panels = [panel.reshape(-1, width, width) for panel in (panel_one, panel_two)]
    each = tuple(panel.shape[0] for panel in panels)
    whole = lax.optimization_barrier(jnp.concatenate([pattern_one, pattern_two]))
    pattern_one, pattern_two = whole[:pattern_one.shape[0]], whole[pattern_one.shape[0]:]
    found_cols = places(steps * cols_grid + q, pattern_one, pattern_two)
    found_rows = places(steps * rows_grid + p, pattern_one, pattern_two)
    found_other = places(steps * rows_grid + (q - p) % rows_grid, pattern_one, pattern_two)
    mine = jnp.concatenate(
        [lax.dynamic_slice_in_dim(panel, p * ROWS, ROWS, 1) for panel in panels], axis=0
    )
    gathered = lax.all_gather(mine, "pcol", axis=0, tiled=True)

    classes = jnp.arange(rows_grid, dtype=jnp.int32)[:, None]
    members = sum(
        jnp.sum((lax.rem(pattern, rows_grid)[None, :] == classes).astype(jnp.int32), axis=1)
        for pattern in (pattern_one, pattern_two)
    )
    fits = jnp.all(members <= FEW)
    def invert(slots, fits, gathered, found_cols, found_other, found_rows, region, link, inv_one, inv_two):
        other, low, high, col_list = pick(slots, each, found_cols, found_other, gathered)
        moves = [
            (a * cols_grid + b, (b - a) % rows_grid * cols_grid + a)
            for a in range(rows_grid) for b in range(cols_grid)
        ]
        rows = lax.ppermute(other, ("prow", "pcol"), moves)
        lows, highs = spread_plane(low, high)
        keep, give, row_list = product(slots, found_rows, col_list, here, region, lows, highs)
        give, rows = lax.optimization_barrier((give, rows))
        got = lax.ppermute(give, "pcol", [(i, i ^ 1) for i in range(cols_grid)])
        parts, fits = sum_along_z(keep, got, fits)
        column_one, column_two, sums = columns(row_list, found_rows, parts, rows, link)
        sums = sum_everywhere(sums, rows_grid, cols_grid)
        diagonal_one, cross_two, diagonal_two = diagonals(sums, link, inv_one, inv_two)
        return (column_one, diagonal_one, column_two, cross_two, diagonal_two), fits

    given = (gathered, found_cols, found_other, found_rows, inverse_region, link_block, inv_diag_one, inv_diag_two)
    outs, fits = invert(FEW, fits, *given)
    return lax.cond(
        fits,
        lambda outs, *given: outs,
        lambda outs, *given: invert(2 * BLOCKS, fits, *given)[0],
        outs, *given,
    )


def solution(mesh):
    return jax.shard_map(
        shards,
        mesh=mesh,
        in_specs=(P(None, "prow", None, "pcol"), P("pcol", None), P("pcol", None), P(), P(), P(), P(), P()),
        out_specs=(P(None, ("prow", "pcol"), None), P(), P(None, ("prow", "pcol"), None), P(), P()),
        check_vma=False,
    )
```
